32 devices in a mesh: dom: 16 (over z, y, x), sub: 2 (over core).
Axes of the slice: x: 2, y: 2, z: 4, core: 2. Of those that a mesh axis runs over, the one named last changes fastest.
Arguments:
- jac_blocks: bfloat16 [384, 6, 128, 128], P(('dom', 'sub')), may hold values from -0.06717514 to 0.06717514
- block_cols: int32 [384, 6], P(('dom', 'sub')), may hold values from 0 to 19, as said below
- precond: float32 [384, 36, 128], P(('dom', 'sub')), may hold values from -0.3 to 0.3
- right_side: float32 [384, 48, 128], P(('dom', 'sub')), may hold values from -6 to 6
- halo_rows: int32 [128, 2], P(('dom', 'sub')), may hold values from 0 to 11
- surface_tile: int32 [256], P(('dom', 'sub')), may hold values from 0 to 11
- surface_block: int32 [256], P(('dom', 'sub')), may hold values from 0 to 7
- surface_count: int32 [32], P(('dom', 'sub')), may hold values from 0 to 8, as said below
- surface_residual_derivative: float32 [256, 18, 128], P(('dom', 'sub')), may hold values from -6 to 6
- lattice_bernstein_weights: bfloat16 [256, 128, 128], P(('dom', 'sub')), may hold values from 0 to 0.03125
Outputs:
- adjoint: float32 [384, 48, 128], P(('dom', 'sub'))
- design_grad: float32 [2, 8, 24, 128], P(None, 'sub')
The draws below stay inside these ranges and needn't reach their ends.
Inputs may be any that keep to these rules, and one draw needn't show every extreme that they name: `block_cols`: entries below 12 name the partition's own tiles; entry 12 + k * 2 + h names halo tile h of neighbour k. `surface_count`: slots at and beyond the count are empty; some partition has all 8 slots live.
All inputs are finite; a program needn't handle non-finite values.
Results may differ from the reference program's by a relative error of at most 0.0055.
Values may be sent and summed in bfloat16 or wider, within the bound.
A program may use at most 64 MiB of HBM per device.

```python
import jax
import jax.numpy as jnp
from jax import lax

NOBJ = 8
NVAR = 6
TILE_CELL_COUNT = 128
CONTROL_PER_BOX = 128
NB = 6
NEIGH = 4
HALO = 2
TILES_DEV = 12
SURF_DEV = 8
FB_DEV = 4
OUTER = 2
INNER = 5
PARTITIONS = 32
TILES = 384
SURFACE_SLOTS = 256
NFB = 8
N_DOM = 16
N_SUB = 2


def draw_jac_blocks(key, part):
    spread = 0.25 * TILE_CELL_COUNT ** (-0.5)
    values = jnp.clip(jax.random.normal(key, (TILES, NB, TILE_CELL_COUNT, TILE_CELL_COUNT), jnp.float32), -3.0, 3.0)
    return (values * spread).astype(jnp.bfloat16)


def draw_precond(key, part):
    values = jnp.clip(jax.random.normal(key, (TILES, NVAR * NVAR, TILE_CELL_COUNT), jnp.float32), -3.0, 3.0)
    return values * 0.1


def draw_block_cols(key, part):
    random_cols = jax.random.randint(key, (TILES, NB - 1), 0, TILES_DEV + NEIGH * HALO)
    local_index = jnp.arange(TILES, dtype=jnp.int32) % TILES_DEV
    forced = TILES_DEV + local_index % (NEIGH * HALO)
    return jnp.concatenate([random_cols.astype(jnp.int32), forced[:, None].astype(jnp.int32)], axis=1)


def draw_surface_count(key, part):
    first_key, second_key, third_key = jax.random.split(key, 3)
    blade = jax.random.randint(first_key, (PARTITIONS,), 0, 4) == 0
    farfield = jax.random.randint(second_key, (PARTITIONS,), 0, SURF_DEV // 4 + 1)
    counts = jnp.where(blade, SURF_DEV, farfield).astype(jnp.int32)
    chosen = jax.random.randint(third_key, (), 0, PARTITIONS)
    return counts.at[chosen].set(SURF_DEV)


def with_ends(values, rng, low, top_value):
    spot = [jax.random.randint(jax.random.fold_in(rng, axis), (), 0, length) for axis, length in enumerate(values.shape)]
    main_axis = values.shape.index(max(values.shape))
    next_to = spot[:main_axis] + [(spot[main_axis] + 1) % values.shape[main_axis]] + spot[main_axis + 1:]
    return values.at[tuple(spot)].set(low).at[tuple(next_to)].set(top_value)


def level_of(key, extent, shards, low, largest):
    loudness, own = 1.0, jax.random.fold_in(key, 6)
    for dim, shards_of in shards:
        steps = jnp.exp(jax.random.uniform(jax.random.fold_in(own, dim), (shards_of,), jnp.float32, low / len(shards), largest / len(shards)))
        loudness = loudness * jnp.repeat(steps, extent[dim] // shards_of).reshape([-1 if axis == dim else 1 for axis in range(len(extent))])
    return loudness


def noise(rng, extent, width, bound, cuts=(), kind=jnp.bfloat16):
    entries = jax.random.normal(rng, extent, jnp.float32) * width
    if len(cuts) > 0:
        entries = level_of(rng, extent, cuts, -0.22, 0.18) * entries
    return jnp.clip(entries, min=-bound, max=bound).astype(kind)


def setup_inputs(seed: int = 0) -> dict:
    keys = jax.random.split(jax.random.key(seed), 11)
    jac_blocks = draw_jac_blocks(jax.random.fold_in(keys[10], 71), 0)
    block_cols = draw_block_cols(jax.random.fold_in(keys[10], 71), 0)
    precond = draw_precond(jax.random.fold_in(keys[10], 71), 0)
    right_side = noise(keys[3], (TILES, NOBJ * NVAR, TILE_CELL_COUNT), 1.0, 6.0, ((0, 32),), jnp.float32)
    halo_rows = with_ends(jax.random.randint(keys[4], (PARTITIONS * NEIGH, HALO), 0, TILES_DEV), jax.random.fold_in(keys[4], 1), 0, TILES_DEV - 1).astype(jnp.int32)
    surface_tile = with_ends(jax.random.randint(keys[5], (SURFACE_SLOTS,), 0, TILES_DEV), jax.random.fold_in(keys[5], 1), 0, TILES_DEV - 1).astype(jnp.int32)
    surface_block = with_ends(jax.random.randint(keys[6], (SURFACE_SLOTS,), 0, NFB), jax.random.fold_in(keys[6], 1), 0, NFB - 1).astype(jnp.int32)
    surface_count = draw_surface_count(jax.random.fold_in(keys[10], 71), 0)
    surface_residual_derivative = noise(keys[8], (SURFACE_SLOTS, NVAR * 3, TILE_CELL_COUNT), 1.0, 6.0, ((0, 32),), jnp.float32)
    lattice_bernstein_weights = jnp.clip(0.03125 * jax.random.uniform(keys[9], (SURFACE_SLOTS, CONTROL_PER_BOX, TILE_CELL_COUNT), jnp.float32) ** level_of(keys[9], (SURFACE_SLOTS, CONTROL_PER_BOX, TILE_CELL_COUNT), ((0, 32),), -0.2, 0.2), 0.0, 0.03125).astype(jnp.bfloat16)
    return {"jac_blocks": jac_blocks, "block_cols": block_cols, "precond": precond, "right_side": right_side, "halo_rows": halo_rows, "surface_tile": surface_tile, "surface_block": surface_block, "surface_count": surface_count, "surface_residual_derivative": surface_residual_derivative, "lattice_bernstein_weights": lattice_bernstein_weights}


OFFSETS = (1, -1, 2, -2)
RELAXATION = 0.7


def variable_mix(blending_factor, residual):
    tile_count = residual.shape[0]
    cell_count = residual.shape[-1]
    residual_split = residual.reshape(tile_count, NOBJ, NVAR, cell_count)
    mixing_split = blending_factor.reshape(tile_count, NVAR, NVAR, cell_count)
    mixed = jnp.sum(mixing_split[:, None, :, :, :] * residual_split[:, :, None, :, :], axis=3)
    return mixed.reshape(tile_count, NOBJ * NVAR, cell_count)


def pick_columns(extended, columns):
    return extended[columns]


def design_gradient(adjoint_flat, surface_tile, surface_block, surface_count, surface_residual_derivative, lattice_bernstein_weights, scaling):
    slot_count = surface_tile.shape[0]
    owner = jnp.arange(slot_count, dtype=jnp.int32) // SURF_DEV
    selected = adjoint_flat[owner * TILES_DEV + surface_tile]
    weights_split = surface_residual_derivative.reshape(slot_count, 1, NVAR, 3, TILE_CELL_COUNT)
    sensitivity = jnp.sum(selected.reshape(slot_count, NOBJ, NVAR, 1, TILE_CELL_COUNT) * weights_split, axis=2)
    alive = (jnp.arange(SURF_DEV, dtype=jnp.int32)[None, :] < surface_count[:, None]).reshape(slot_count)
    alive = alive.astype(jnp.float32)
    rounded = (sensitivity * alive[:, None, None, None]).reshape(slot_count, NOBJ * 3, TILE_CELL_COUNT).astype(jnp.bfloat16)
    projected = jnp.einsum("uoc,upc->uop", rounded.astype(jnp.float32), lattice_bernstein_weights.astype(jnp.float32))
    summed = jax.ops.segment_sum(projected, surface_block, num_segments=FB_DEV * N_SUB)
    return summed * scaling


def reference(jac_blocks, block_cols, precond, right_side, halo_rows, surface_tile, surface_block, surface_count, surface_residual_derivative, lattice_bernstein_weights):
    partitions = N_DOM * N_SUB
    row_count = NOBJ * NVAR
    blocks = jac_blocks.reshape(partitions, TILES_DEV, NB, TILE_CELL_COUNT, TILE_CELL_COUNT)
    columns = block_cols.reshape(partitions, TILES_DEV, NB)
    blending_factor = precond.reshape(partitions, TILES_DEV, NVAR * NVAR, TILE_CELL_COUNT)
    targets = right_side.reshape(partitions, TILES_DEV, row_count, TILE_CELL_COUNT)
    demanded_items = halo_rows.reshape(partitions, len(OFFSETS), HALO)
    device_ids = jnp.arange(partitions, dtype=jnp.int32)
    group = device_ids // N_SUB
    member = device_ids % N_SUB
    offset_table = jnp.array(OFFSETS, dtype=jnp.int32)
    source = ((group[:, None] - offset_table[None, :]) % N_DOM) * N_SUB + member[:, None]
    halo_global = (source[:, :, None] * TILES_DEV + demanded_items).reshape(partitions, len(OFFSETS) * HALO)
    local_global = device_ids[:, None] * TILES_DEV + jnp.arange(TILES_DEV, dtype=jnp.int32)[None, :]
    extended_global = jnp.concatenate([local_global, halo_global], axis=1).astype(jnp.int32)
    column_global = jax.vmap(pick_columns)(extended_global, columns)
    adjoint = jnp.zeros((partitions, TILES_DEV, row_count, TILE_CELL_COUNT), jnp.float32)
    scaling = (FB_DEV / (SURF_DEV * N_DOM)) ** 0.5
    gradients = []
    for outer_index in range(OUTER):
        for sweep_index in range(INNER):
            rounded = adjoint.astype(jnp.bfloat16).reshape(partitions * TILES_DEV, row_count, TILE_CELL_COUNT)

            def device_sweep(packed):
                block_set, column_set, current, target, mixing_set = packed
                picked = rounded[column_set].astype(jnp.float32)
                coupled = current + jnp.einsum("tbor,tbrc->toc", picked, block_set.astype(jnp.float32))
                residual = target - coupled
                return current + RELAXATION * residual + variable_mix(mixing_set, residual)

            adjoint = lax.map(device_sweep, (blocks, column_global, adjoint, targets, blending_factor))
        adjoint_flat = adjoint.reshape(partitions * TILES_DEV, row_count, TILE_CELL_COUNT)
        gradients.append(design_gradient(adjoint_flat, surface_tile, surface_block, surface_count, surface_residual_derivative, lattice_bernstein_weights, scaling))
    return adjoint.reshape(partitions * TILES_DEV, row_count, TILE_CELL_COUNT), jnp.stack(gradients, axis=0)
```

```python
import functools
import math

import jax
import jax.numpy as jnp
from jax import lax
from jax.experimental import pallas as pl
from jax.experimental.pallas import tpu as pltpu
from jax.sharding import PartitionSpec as P

NOBJ = 8
NVAR = 6
NDIR = 3
OUTER = 2
INNER = 5

OFFSETS = (1, -1, 2, -2)
RELAXATION = 0.7
MESH = pl.DeviceIdType.MESH


def mixed(pre_ref, tile, residual):
    out = []
    for v in range(NVAR):
        total = RELAXATION * residual[v]
        for w in range(NVAR):
            total = total + pre_ref[tile, pl.ds(v * NVAR + w, 1), :] * residual[w]
        out.append(total)
    return out


def kernel(
    n_dom, n_sub, scaling,
    jac_hbm, pre_hbm, rhs_hbm, srd_hbm, weights_hbm,
    cols_ref, halo_ref, surf_tile_ref, surf_block_ref, count_ref,
    adj_out, grad_out,
    jac_ref, pre_ref, rhs_in, srd_ref, weights_ref,
    rhs_ref, adj_ref, ext_ref, send_buf, recv_buf,
    want_out, want_in, want_ref,
    part_ref, sub_buf, acc_ref, dom_buf,
    load_sem, want_send, want_recv, want_local, halo_send, halo_recv,
    sub_send, sub_recv, dom_send, dom_recv,
):
    tiles = adj_ref.shape[0]
    blocks = cols_ref.shape[0] // tiles
    cells = adj_ref.shape[-1]
    halo = recv_buf.shape[2]
    slots = srd_ref.shape[0]
    fb_dev = grad_out.shape[1]
    rows = NOBJ * NVAR
    a = lax.axis_index("dom")
    s = lax.axis_index("sub")

    def shifted(offset):
        return lax.rem(a + offset + n_dom, n_dom)

    loads = [
        pltpu.make_async_copy(src, dst, load_sem.at[number])
        for number, (src, dst) in enumerate((
            (rhs_hbm, rhs_in), (pre_hbm, pre_ref), (jac_hbm, jac_ref),
            (srd_hbm, srd_ref), (weights_hbm, weights_ref)))
    ]
    for load in loads:
        load.start()

    dom_steps = n_dom.bit_length() - 1
    partners = [a + 2 ** k * (1 - 2 * lax.rem(a // 2 ** k, 2)) for k in range(dom_steps)]
    greet = [(shifted(offset), s) for offset in OFFSETS]
    greet += [(partners[k], s) for k in range(2, dom_steps)]
    greet += [(a, lax.rem(s + d, n_sub)) for d in range(1, n_sub)]
    barrier = pltpu.get_barrier_semaphore()
    for device in greet:
        pl.semaphore_signal(barrier, inc=1, device_id=device, device_id_type=MESH)

    lane = lax.broadcasted_iota(jnp.int32, want_out.shape[1:], 1)
    for k in range(len(OFFSETS)):
        demand = jnp.zeros(want_out.shape[1:], jnp.int32)
        for h in range(halo):
            demand = jnp.where(lane == h, halo_ref[k * halo + h], demand)
        want_out[k] = demand
    pl.semaphore_wait(barrier, len(greet))

    def want_copy(k):
        return pltpu.make_async_remote_copy(
            src_ref=want_out.at[k], dst_ref=want_in.at[k],
            send_sem=want_send.at[k], recv_sem=want_recv.at[k],
            device_id=(shifted(-OFFSETS[k]), s), device_id_type=MESH)

    for k in range(len(OFFSETS)):
        want_copy(k).start()

    loads[0].wait()
    loads[1].wait()

    def first(i, carry):
        residual = []
        for v in range(NVAR):
            value = rhs_in[i, pl.ds(v, NOBJ, stride=NVAR), :]
            rhs_ref[i, v] = value
            residual.append(value)
        for v, change in enumerate(mixed(pre_ref, i, residual)):
            adj_ref[i, v] = change
        return carry

    lax.fori_loop(0, tiles, first, 0)

    for k in range(len(OFFSETS)):
        want_copy(k).wait()
    to_smem = pltpu.make_async_copy(want_in, want_ref, want_local)
    to_smem.start()
    to_smem.wait()
    loads[2].wait()

    def sweep(number, between=None):
        parity = lax.rem(number, 2)

        def halo_copy(k):
            return pltpu.make_async_remote_copy(
                src_ref=send_buf.at[k], dst_ref=recv_buf.at[parity, k],
                send_sem=halo_send.at[k], recv_sem=halo_recv.at[parity, k],
                device_id=(shifted(OFFSETS[k]), s), device_id_type=MESH)

        for k in (3, 2, 1, 0):
            for h in range(halo):
                tile = adj_ref[want_ref[k, 0, h]]
                send_buf[k, h] = tile.reshape(rows, cells).astype(jnp.bfloat16)
            halo_copy(k).start()
        for i in range(tiles):
            ext_ref[i] = adj_ref[i].reshape(rows, cells).astype(jnp.bfloat16)
        if between is not None:
            between()
        for k in range(len(OFFSETS)):
            halo_copy(k).wait()
            for h in range(halo):
                ext_ref[tiles + k * halo + h] = recv_buf[parity, k, h]

        group = math.gcd(tiles, 4)

        def some(g, carry):
            for sub_tile in range(group):
                i = g * group + sub_tile
                picked = jnp.concatenate(
                    [ext_ref[cols_ref[i * blocks + b]] for b in range(blocks)], axis=1)
                product = jnp.dot(picked, jac_ref[i], preferred_element_type=jnp.float32)
                current = [adj_ref[i, v] for v in range(NVAR)]
                residual = [
                    rhs_ref[i, v] - (current[v] + product[v * NOBJ:(v + 1) * NOBJ])
                    for v in range(NVAR)
                ]
                for v, change in enumerate(mixed(pre_ref, i, residual)):
                    adj_ref[i, v] = current[v] + change
            return carry

        lax.fori_loop(0, tiles // group, some, 0)

    def design(iteration):
        projected = []
        for u in range(slots):
            alive = jnp.where(u < count_ref[0], 1.0, 0.0).astype(jnp.float32)
            selected = adj_ref[surf_tile_ref[u]]
            parts = []
            for k in range(NDIR):
                total = selected[0] * srd_ref[u, pl.ds(k, 1), :]
                for v in range(1, NVAR):
                    total = total + selected[v] * srd_ref[u, pl.ds(v * NDIR + k, 1), :]
                parts.append(total * alive)
            rounded = jnp.concatenate(parts, axis=0).astype(jnp.bfloat16)
            projected.append(lax.dot_general(
                rounded, weights_ref[u], (((1,), (1,)), ((), ())),
                preferred_element_type=jnp.float32))
        for owner in range(n_sub):
            for f in range(fb_dev):
                total = jnp.zeros_like(projected[0])
                for u in range(slots):
                    chosen = jnp.where(surf_block_ref[u] == owner * fb_dev + f, 1.0, 0.0)
                    total = total + chosen.astype(jnp.float32) * projected[u]
                part_ref[owner, iteration, f] = total

    def looped(number, carry):
        sweep(number)
        return carry

    lax.fori_loop(0, INNER - 1, looped, 0)
    loads[3].wait()
    loads[4].wait()
    sweep(INNER - 1, lambda: design(0))
    lax.fori_loop(INNER, 2 * INNER - 1, looped, 0)
    design(1)

    def sub_copy(d):
        other = lax.rem(s + d, n_sub)
        return pltpu.make_async_remote_copy(
            src_ref=part_ref.at[other], dst_ref=sub_buf.at[d - 1],
            send_sem=sub_send.at[d - 1], recv_sem=sub_recv.at[d - 1],
            device_id=(a, other), device_id_type=MESH)

    def dom_copy(k):
        return pltpu.make_async_remote_copy(
            src_ref=acc_ref.at[k], dst_ref=dom_buf.at[k],
            send_sem=dom_send.at[k], recv_sem=dom_recv.at[k],
            device_id=(partners[k], s), device_id_type=MESH)

    for d in range(1, n_sub):
        sub_copy(d).start()
    for i in range(tiles):
        for v in range(NVAR):
            adj_out[i, pl.ds(v, NOBJ, stride=NVAR), :] = adj_ref[i, v]
    total = part_ref[s]
    for d in range(1, n_sub):
        sub_copy(d).wait()
        total = total + sub_buf[d - 1]
    for k in range(dom_steps):
        acc_ref[k] = total
        dom_copy(k).start()
        dom_copy(k).wait()
        total = acc_ref[k] + dom_buf[k]
    total = total * scaling
    for iteration in range(OUTER):
        for f in range(fb_dev):
            for k in range(NDIR):
                grad_out[iteration, f, pl.ds(k, NOBJ, stride=NDIR), :] = (
                    total[iteration, f, k * NOBJ:(k + 1) * NOBJ])


def per_device(
    n_dom,
    n_sub,
    block_total,
    jac_blocks,
    block_cols,
    precond,
    right_side,
    halo_rows,
    surface_tile,
    surface_block,
    surface_count,
    surface_residual_derivative,
    lattice_bernstein_weights,
):
    tiles, blocks, cells, _ = jac_blocks.shape
    slots, controls, _ = lattice_bernstein_weights.shape
    neighbours, halo = halo_rows.shape
    fb_dev = block_total // n_sub
    rows = NOBJ * NVAR
    scaling = math.sqrt(fb_dev / (slots * n_dom))
    dom_steps = n_dom.bit_length() - 1
    grad_rows = NOBJ * NDIR
    f32, bf16, i32 = jnp.float32, jnp.bfloat16, jnp.int32
    dma = pltpu.SemaphoreType.DMA
    anywhere = pl.BlockSpec(memory_space=pl.ANY)
    scalars = pl.BlockSpec(memory_space=pltpu.SMEM)
    vmem = pl.BlockSpec(memory_space=pltpu.VMEM)
    return pl.pallas_call(
        functools.partial(kernel, n_dom, n_sub, scaling),
        out_shape=(
            jax.ShapeDtypeStruct((tiles, rows, cells), f32),
            jax.ShapeDtypeStruct((OUTER, fb_dev, grad_rows, controls), f32),
        ),
        in_specs=[anywhere] * 5 + [scalars] * 5,
        out_specs=(vmem, vmem),
        scratch_shapes=[
            pltpu.VMEM((tiles, blocks * cells, cells), bf16),
            pltpu.VMEM(precond.shape, f32),
            pltpu.VMEM(right_side.shape, f32),
            pltpu.VMEM(surface_residual_derivative.shape, f32),
            pltpu.VMEM(lattice_bernstein_weights.shape, bf16),
            pltpu.VMEM((tiles, NVAR, NOBJ, cells), f32),
            pltpu.VMEM((tiles, NVAR, NOBJ, cells), f32),
            pltpu.VMEM((tiles + neighbours * halo, rows, cells), bf16),
            pltpu.VMEM((neighbours, halo, rows, cells), bf16),
            pltpu.VMEM((2, neighbours, halo, rows, cells), bf16),
            pltpu.VMEM((neighbours, 8, 128), i32),
            pltpu.VMEM((neighbours, 8, 128), i32),
            pltpu.SMEM((neighbours, 8, 128), i32),
            pltpu.VMEM((n_sub, OUTER, fb_dev, grad_rows, controls), f32),
            pltpu.VMEM((n_sub - 1, OUTER, fb_dev, grad_rows, controls), f32),
            pltpu.VMEM((dom_steps, OUTER, fb_dev, grad_rows, controls), f32),
            pltpu.VMEM((dom_steps, OUTER, fb_dev, grad_rows, controls), f32),
            dma((5,)),
            dma((neighbours,)),
            dma((neighbours,)),
            dma,
            dma((neighbours,)),
            dma((2, neighbours)),
            dma((n_sub - 1,)),
            dma((n_sub - 1,)),
            dma((dom_steps,)),
            dma((dom_steps,)),
        ],
        compiler_params=pltpu.CompilerParams(
            collective_id=0, has_side_effects=True, vmem_limit_bytes=40 * 1024 * 1024),
    )(
        jac_blocks.reshape(tiles, blocks * cells, cells),
        precond,
        right_side,
        surface_residual_derivative,
        lattice_bernstein_weights,
        block_cols.reshape(-1),
        halo_rows.reshape(-1),
        surface_tile,
        surface_block,
        surface_count,
    )


FB_DEV = 4


def solution(mesh):
    n_dom, n_sub = mesh.shape["dom"], mesh.shape["sub"]
    both = ("dom", "sub")
    in_specs = (
        P(both, None, None, None),
        P(both, None),
        P(both, None, None),
        P(both, None, None),
        P(both, None),
        P(both),
        P(both),
        P(both),
        P(both, None, None),
        P(both, None, None),
    )
    out_specs = (P(both, None, None), P(None, "sub", None, None))
    return jax.shard_map(
        functools.partial(per_device, n_dom, n_sub, FB_DEV * n_sub),
        mesh=mesh, in_specs=in_specs, out_specs=out_specs, check_vma=False,
    )
```

```python
import functools
import math

import jax
import jax.numpy as jnp
from jax import lax
from jax.experimental import pallas as pl
from jax.experimental.pallas import tpu as pltpu
from jax.sharding import PartitionSpec as P

NOBJ = 8
NVAR = 6
NDIR = 3
OUTER = 2
INNER = 5

OFFSETS = (1, -1, 2, -2)
RELAXATION = 0.7
MESH = pl.DeviceIdType.MESH


def mixed(pre_ref, tile, residual):
    out = []
    for v in range(NVAR):
        total = RELAXATION * residual[v]
        for w in range(NVAR):
            total = total + pre_ref[tile, pl.ds(v * NVAR + w, 1), :] * residual[w]
        out.append(total)
    return out


def kernel(
    n_dom, n_sub, scaling,
    jac_hbm, pre_hbm, rhs_hbm, srd_hbm, weights_hbm,
    cols_hbm, halo_hbm, surf_tile_hbm, surf_block_hbm, count_hbm,
    adj_out, grad_out,
    jac_ref, pre_ref, rhs_in, srd_ref, weights_ref,
    cols_ref, halo_ref, surf_tile_ref, surf_block_ref, count_ref,
    rhs_ref, adj_ref, ext_ref, send_buf, recv_buf,
    want_out, want_in, want_ref,
    part_ref, sub_buf, acc_ref, dom_buf,
    load_sem, want_send, want_recv, want_local, halo_send, halo_recv,
    sub_send, sub_recv, dom_send, dom_recv,
):
    blocks, tiles = cols_ref.shape
    cells = adj_ref.shape[-1]
    halo = recv_buf.shape[2]
    slots = weights_ref.shape[0]
    fb_dev = grad_out.shape[1]
    rows = NOBJ * NVAR
    last = OUTER * INNER - 1
    neighbours = range(len(OFFSETS))
    a = lax.axis_index("dom")
    s = lax.axis_index("sub")

    def shifted(offset):
        return lax.rem(a + offset + n_dom, n_dom)

    pairs = {
        "halo": (halo_hbm, halo_ref), "rhs": (rhs_hbm, rhs_in), "pre": (pre_hbm, pre_ref),
        "cols": (cols_hbm, cols_ref), "jac": (jac_hbm, jac_ref),
        "srd": (srd_hbm, srd_ref), "weights": (weights_hbm, weights_ref),
        "tile": (surf_tile_hbm, surf_tile_ref), "block": (surf_block_hbm, surf_block_ref),
        "count": (count_hbm, count_ref),
    }
    loads = {}
    for number, (name, (src, dst)) in enumerate(pairs.items()):
        loads[name] = pltpu.make_async_copy(src, dst, load_sem.at[number])

    dom_steps = n_dom.bit_length() - 1
    partners = [a + 2 ** k * (1 - 2 * lax.rem(a // 2 ** k, 2)) for k in range(dom_steps)]
    greet = [(shifted(offset), s) for offset in OFFSETS]
    greet += [(partners[k], s) for k in range(2, dom_steps)]
    greet += [(a, lax.rem(s + d, n_sub)) for d in range(1, n_sub)]
    barrier = pltpu.get_barrier_semaphore()
    for device in greet:
        pl.semaphore_signal(barrier, inc=1, device_id=device, device_id_type=MESH)
    for load in loads.values():
        load.start()

    loads["halo"].wait()
    lane = lax.broadcasted_iota(jnp.int32, want_out.shape[1:], 1)
    for k in neighbours:
        demand = jnp.zeros(want_out.shape[1:], jnp.int32)
        for h in range(halo):
            demand = jnp.where(lane == h, halo_ref[h, k], demand)
        want_out[k] = demand
    pl.semaphore_wait(barrier, len(greet))

    def want_copy(k):
        return pltpu.make_async_remote_copy(
            src_ref=want_out.at[k], dst_ref=want_in.at[k],
            send_sem=want_send.at[k], recv_sem=want_recv.at[k],
            device_id=(shifted(-OFFSETS[k]), s), device_id_type=MESH)

    for k in neighbours:
        want_copy(k).start()

    loads["rhs"].wait()
    loads["pre"].wait()

    def first(i, carry):
        residual = []
        for v in range(NVAR):
            value = rhs_in[i, pl.ds(v, NOBJ, stride=NVAR), :]
            rhs_ref[i, v] = value
            residual.append(value)
        for v, change in enumerate(mixed(pre_ref, i, residual)):
            adj_ref[i, v] = change
        return carry

    lax.fori_loop(0, tiles, first, 0)

    def halo_copy(number, k):
        parity = lax.rem(number, 2)
        return pltpu.make_async_remote_copy(
            src_ref=send_buf.at[parity, k], dst_ref=recv_buf.at[parity, k],
            send_sem=halo_send.at[parity, k], recv_sem=halo_recv.at[parity, k],
            device_id=(shifted(OFFSETS[k]), s), device_id_type=MESH)

    def round_own():
        for i in range(tiles):
            ext_ref[i] = adj_ref[i].reshape(rows, cells).astype(jnp.bfloat16)

    for k in neighbours:
        want_copy(k).wait()
    to_smem = pltpu.make_async_copy(want_in, want_ref, want_local)
    to_smem.start()
    to_smem.wait()
    for k in neighbours:
        for h in range(halo):
            tile = adj_ref[want_ref[k, 0, h]]
            send_buf[1, k, h] = tile.reshape(rows, cells).astype(jnp.bfloat16)
        halo_copy(1, k).start()
    round_own()
    for name in ("cols", "jac", "srd", "weights", "tile", "block", "count"):
        loads[name].wait()

    def updated(i):
        picked = jnp.concatenate([ext_ref[cols_ref[b, i]] for b in range(blocks)], axis=1)
        product = jnp.dot(picked, jac_ref[i], preferred_element_type=jnp.float32)
        current = [adj_ref[i, v] for v in range(NVAR)]
        residual = [
            rhs_ref[i, v] - (current[v] + product[v * NOBJ:(v + 1) * NOBJ]) for v in range(NVAR)
        ]
        return [c + change for c, change in zip(current, mixed(pre_ref, i, residual))]

    group = math.gcd(tiles, 4)

    def some(g, carry):
        fresh = [updated(g * group + t) for t in range(group)]
        for t in range(group):
            for v in range(NVAR):
                adj_ref[g * group + t, v] = fresh[t][v]
        return carry

    def receive(number):
        parity = lax.rem(number, 2)
        for k in neighbours:
            halo_copy(number, k).wait()
        for k in neighbours:
            for h in range(halo):
                ext_ref[tiles + k * halo + h] = recv_buf[parity, k, h]

    def design(iteration):
        projected = []
        for u in range(slots):
            alive = jnp.where(u < count_ref[0], 1.0, 0.0).astype(jnp.float32)
            selected = adj_ref[surf_tile_ref[u]]
            parts = []
            for k in range(NDIR):
                total = selected[0] * srd_ref[k, pl.ds(u, 1), :]
                for v in range(1, NVAR):
                    total = total + selected[v] * srd_ref[v * NDIR + k, pl.ds(u, 1), :]
                parts.append(total * alive)
            rounded = jnp.concatenate(parts, axis=0).astype(jnp.bfloat16)
            projected.append(lax.dot_general(
                rounded, weights_ref[u], (((1,), (1,)), ((), ())),
                preferred_element_type=jnp.float32))
        for owner in range(n_sub):
            for f in range(fb_dev):
                total = jnp.zeros_like(projected[0])
                for u in range(slots):
                    chosen = jnp.where(surf_block_ref[u] == owner * fb_dev + f, 1.0, 0.0)
                    total = total + chosen.astype(jnp.float32) * projected[u]
                part_ref[owner, f, iteration] = total

    def sweep(number, carry):
        receive(number)
        for some_neighbours in (neighbours[:2], neighbours[2:]):
            for k in some_neighbours:
                for h in range(halo):
                    fresh = jnp.concatenate(updated(want_ref[k, 0, h]), axis=0)
                    send_buf[lax.rem(number + 1, 2), k, h] = fresh.astype(jnp.bfloat16)
            for k in some_neighbours:
                halo_copy(number + 1, k).start()
        lax.fori_loop(0, tiles // group, some, 0)
        round_own()

        @pl.when(number == INNER - 1)
        def _():
            design(0)

        return carry

    lax.fori_loop(1, last, sweep, 0)
    receive(last)
    lax.fori_loop(0, tiles // group, some, 0)
    design(1)

    def sub_copy(d, f):
        other = lax.rem(s + d, n_sub)
        return pltpu.make_async_remote_copy(
            src_ref=part_ref.at[other, f], dst_ref=sub_buf.at[d - 1, f],
            send_sem=sub_send.at[d - 1, f], recv_sem=sub_recv.at[d - 1, f],
            device_id=(a, other), device_id_type=MESH)

    def dom_copy(k, f):
        return pltpu.make_async_remote_copy(
            src_ref=acc_ref.at[k, f], dst_ref=dom_buf.at[k, f],
            send_sem=dom_send.at[k, f], recv_sem=dom_recv.at[k, f],
            device_id=(partners[(k + f) % dom_steps], s), device_id_type=MESH)

    for f in range(fb_dev):
        for d in range(1, n_sub):
            sub_copy(d, f).start()
    for f in range(fb_dev):
        total = part_ref[s, f]
        for d in range(1, n_sub):
            sub_copy(d, f).wait()
            total = total + sub_buf[d - 1, f]
        acc_ref[0, f] = total
        dom_copy(0, f).start()
    for i in range(tiles):
        for v in range(NVAR):
            adj_out[i, pl.ds(v, NOBJ, stride=NVAR), :] = adj_ref[i, v]
    for k in range(dom_steps):
        for f in range(fb_dev):
            dom_copy(k, f).wait()
            total = acc_ref[k, f] + dom_buf[k, f]
            if k < dom_steps - 1:
                acc_ref[k + 1, f] = total
                dom_copy(k + 1, f).start()
            else:
                total = total * scaling
                for iteration in range(OUTER):
                    for x in range(NDIR):
                        grad_out[iteration, f, pl.ds(x, NOBJ, stride=NDIR), :] = (
                            total[iteration, x * NOBJ:(x + 1) * NOBJ])


def per_device(
    n_dom,
    n_sub,
    block_total,
    jac_blocks,
    block_cols,
    precond,
    right_side,
    halo_rows,
    surface_tile,
    surface_block,
    surface_count,
    surface_residual_derivative,
    lattice_bernstein_weights,
):
    tiles, blocks, cells, _ = jac_blocks.shape
    slots, controls, _ = lattice_bernstein_weights.shape
    neighbours, halo = halo_rows.shape
    fb_dev = block_total // n_sub
    rows = NOBJ * NVAR
    scaling = math.sqrt(fb_dev / (slots * n_dom))
    dom_steps = n_dom.bit_length() - 1
    grad_rows = NOBJ * NDIR
    f32, bf16, i32 = jnp.float32, jnp.bfloat16, jnp.int32
    dma = pltpu.SemaphoreType.DMA
    operands = (
        jac_blocks.reshape(tiles, blocks * cells, cells),
        precond,
        right_side,
        jnp.swapaxes(surface_residual_derivative, 0, 1),
        lattice_bernstein_weights,
        block_cols.T,
        halo_rows.T,
        surface_tile,
        surface_block,
        surface_count,
    )
    vmem = pl.BlockSpec(memory_space=pltpu.VMEM)
    return pl.pallas_call(
        functools.partial(kernel, n_dom, n_sub, scaling),
        out_shape=(
            jax.ShapeDtypeStruct((tiles, rows, cells), f32),
            jax.ShapeDtypeStruct((OUTER, fb_dev, grad_rows, controls), f32),
        ),
        in_specs=[pl.BlockSpec(memory_space=pltpu.HBM)] * len(operands),
        out_specs=(vmem, vmem),
        scratch_shapes=[pltpu.VMEM(x.shape, x.dtype) for x in operands[:5]]
        + [pltpu.SMEM(x.shape, x.dtype) for x in operands[5:]]
        + [
            pltpu.VMEM((tiles, NVAR, NOBJ, cells), f32),
            pltpu.VMEM((tiles, NVAR, NOBJ, cells), f32),
            pltpu.VMEM((tiles + neighbours * halo, rows, cells), bf16),
            pltpu.VMEM((2, neighbours, halo, rows, cells), bf16),
            pltpu.VMEM((2, neighbours, halo, rows, cells), bf16),
            pltpu.VMEM((neighbours, 8, 128), i32),
            pltpu.VMEM((neighbours, 8, 128), i32),
            pltpu.SMEM((neighbours, 8, 128), i32),
            pltpu.VMEM((n_sub, fb_dev, OUTER, grad_rows, controls), f32),
            pltpu.VMEM((n_sub - 1, fb_dev, OUTER, grad_rows, controls), f32),
            pltpu.VMEM((dom_steps, fb_dev, OUTER, grad_rows, controls), f32),
            pltpu.VMEM((dom_steps, fb_dev, OUTER, grad_rows, controls), f32),
            dma((len(operands),)),
            dma((neighbours,)),
            dma((neighbours,)),
            dma,
            dma((2, neighbours)),
            dma((2, neighbours)),
            dma((n_sub - 1, fb_dev)),
            dma((n_sub - 1, fb_dev)),
            dma((dom_steps, fb_dev)),
            dma((dom_steps, fb_dev)),
        ],
        compiler_params=pltpu.CompilerParams(
            collective_id=0, has_side_effects=True, vmem_limit_bytes=60 * 1024 * 1024),
    )(*operands)


FB_DEV = 4


def solution(mesh):
    n_dom, n_sub = mesh.shape["dom"], mesh.shape["sub"]
    both = ("dom", "sub")
    in_specs = (
        P(both, None, None, None),
        P(both, None),
        P(both, None, None),
        P(both, None, None),
        P(both, None),
        P(both),
        P(both),
        P(both),
        P(both, None, None),
        P(both, None, None),
    )
    out_specs = (P(both, None, None), P(None, "sub", None, None))
    return jax.shard_map(
        functools.partial(per_device, n_dom, n_sub, FB_DEV * n_sub),
        mesh=mesh, in_specs=in_specs, out_specs=out_specs, check_vma=False,
    )
```

```python
import functools
import math

import jax
import jax.numpy as jnp
from jax import lax
from jax.experimental import pallas as pl
from jax.experimental.pallas import tpu as pltpu
from jax.sharding import PartitionSpec as P

NOBJ = 8
NVAR = 6
NDIR = 3
OUTER = 2
INNER = 5

OFFSETS = (1, -1, 2, -2)
RELAXATION = 0.7
MESH = pl.DeviceIdType.MESH


def mixed(pre_ref, tile, residual):
    out = []
    for v in range(NVAR):
        total = RELAXATION * residual[v]
        for w in range(NVAR):
            total = total + pre_ref[tile, v * NVAR + w] * residual[w]
        out.append(total)
    return out


def kernel(
    n_dom, n_sub, scaling,
    jac_hbm, pre_hbm, rhs_hbm, srd_hbm, weights_hbm,
    cols_hbm, halo_hbm, surf_tile_hbm, surf_block_hbm, count_hbm,
    adj_out, grad_out,
    jac_ref, pre_in, rhs_in, srd_ref, weights_ref,
    cols_ref, halo_ref, surf_tile_ref, surf_block_ref, count_ref,
    pre_ref, rhs_ref, adj_ref, ext_ref, send_buf, recv_buf,
    want_out, want_in, want_ref,
    part_ref, sub_buf, acc_ref, dom_buf,
    load_sem, want_send, want_recv, want_local, halo_send, halo_recv,
    sub_send, sub_recv, dom_send, dom_recv,
):
    blocks, tiles = cols_ref.shape
    cells = adj_ref.shape[-1]
    halo = recv_buf.shape[2]
    slots = weights_ref.shape[0]
    fb_dev = grad_out.shape[1]
    rows = NOBJ * NVAR
    last = OUTER * INNER - 1
    neighbours = range(len(OFFSETS))
    a = lax.axis_index("dom")
    s = lax.axis_index("sub")

    def shifted(offset):
        return lax.rem(a + offset + n_dom, n_dom)

    pairs = {
        "halo": (halo_hbm, halo_ref), "rhs": (rhs_hbm, rhs_in), "pre": (pre_hbm, pre_in),
        "cols": (cols_hbm, cols_ref), "jac": (jac_hbm, jac_ref),
        "srd": (srd_hbm, srd_ref), "weights": (weights_hbm, weights_ref),
        "tile": (surf_tile_hbm, surf_tile_ref), "block": (surf_block_hbm, surf_block_ref),
        "count": (count_hbm, count_ref),
    }
    loads = {}
    for number, (name, (src, dst)) in enumerate(pairs.items()):
        loads[name] = pltpu.make_async_copy(src, dst, load_sem.at[number])

    dom_steps = n_dom.bit_length() - 1
    partners = [a + 2 ** k * (1 - 2 * lax.rem(a // 2 ** k, 2)) for k in range(dom_steps)]
    greet = [(shifted(offset), s) for offset in OFFSETS]
    greet += [(partners[k], s) for k in range(2, dom_steps)]
    greet += [(a, lax.rem(s + d, n_sub)) for d in range(1, n_sub)]
    barrier = pltpu.get_barrier_semaphore()
    for device in greet:
        pl.semaphore_signal(barrier, inc=1, device_id=device, device_id_type=MESH)
    for load in loads.values():
        load.start()

    loads["halo"].wait()
    lane = lax.broadcasted_iota(jnp.int32, want_out.shape[1:], 1)
    for k in neighbours:
        demand = jnp.zeros(want_out.shape[1:], jnp.int32)
        for h in range(halo):
            demand = jnp.where(lane == h, halo_ref[h, k], demand)
        want_out[k] = demand
    pl.semaphore_wait(barrier, len(greet))

    def want_copy(k):
        return pltpu.make_async_remote_copy(
            src_ref=want_out.at[k], dst_ref=want_in.at[k],
            send_sem=want_send.at[k], recv_sem=want_recv.at[k],
            device_id=(shifted(-OFFSETS[k]), s), device_id_type=MESH)

    for k in neighbours:
        want_copy(k).start()

    loads["rhs"].wait()
    loads["pre"].wait()

    def first(i, carry):
        for row in range(NVAR * NVAR):
            spread = jnp.broadcast_to(pre_in[i, pl.ds(row, 1), :], (NOBJ, cells))
            pre_ref[i, row] = spread
        residual = []
        for v in range(NVAR):
            value = rhs_in[i, pl.ds(v, NOBJ, stride=NVAR), :]
            rhs_ref[i, v] = value
            residual.append(value)
        for v, change in enumerate(mixed(pre_ref, i, residual)):
            adj_ref[i, v] = change
        return carry

    lax.fori_loop(0, tiles, first, 0)

    def halo_copy(number, k):
        parity = lax.rem(number, 2)
        return pltpu.make_async_remote_copy(
            src_ref=send_buf.at[parity, k], dst_ref=recv_buf.at[parity, k],
            send_sem=halo_send.at[parity, k], recv_sem=halo_recv.at[parity, k],
            device_id=(shifted(OFFSETS[k]), s), device_id_type=MESH)

    def round_own():
        for i in range(tiles):
            ext_ref[i] = adj_ref[i].reshape(rows, cells).astype(jnp.bfloat16)

    for k in neighbours:
        want_copy(k).wait()
    to_smem = pltpu.make_async_copy(want_in, want_ref, want_local)
    to_smem.start()
    to_smem.wait()
    for k in neighbours:
        for h in range(halo):
            tile = adj_ref[want_ref[k, 0, h]]
            send_buf[1, k, h] = tile.reshape(rows, cells).astype(jnp.bfloat16)
        halo_copy(1, k).start()
    round_own()
    for name in ("cols", "jac", "srd", "weights", "tile", "block", "count"):
        loads[name].wait()

    def updated(i):
        picked = jnp.concatenate([ext_ref[cols_ref[b, i]] for b in range(blocks)], axis=1)
        product = jnp.dot(picked, jac_ref[i], preferred_element_type=jnp.float32)
        current = [adj_ref[i, v] for v in range(NVAR)]
        residual = [
            rhs_ref[i, v] - (current[v] + product[v * NOBJ:(v + 1) * NOBJ]) for v in range(NVAR)
        ]
        return [c + change for c, change in zip(current, mixed(pre_ref, i, residual))]

    def update_own():
        for i in range(tiles):
            for v, value in enumerate(updated(i)):
                adj_ref[i, v] = value

    def receive(number):
        parity = lax.rem(number, 2)
        for k in neighbours:
            halo_copy(number, k).wait()
        for k in neighbours:
            for h in range(halo):
                ext_ref[tiles + k * halo + h] = recv_buf[parity, k, h]

    def design(iteration):
        projected = []
        for u in range(slots):
            alive = jnp.where(u < count_ref[0], 1.0, 0.0).astype(jnp.float32)
            selected = adj_ref[surf_tile_ref[u]]
            parts = []
            for k in range(NDIR):
                total = selected[0] * srd_ref[k, pl.ds(u, 1), :]
                for v in range(1, NVAR):
                    total = total + selected[v] * srd_ref[v * NDIR + k, pl.ds(u, 1), :]
                parts.append(total * alive)
            rounded = jnp.concatenate(parts, axis=0).astype(jnp.bfloat16)
            projected.append(lax.dot_general(
                rounded, weights_ref[u], (((1,), (1,)), ((), ())),
                preferred_element_type=jnp.float32))
        for owner in range(n_sub):
            for f in range(fb_dev):
                total = jnp.zeros_like(projected[0])
                for u in range(slots):
                    chosen = jnp.where(surf_block_ref[u] == owner * fb_dev + f, 1.0, 0.0)
                    total = total + chosen.astype(jnp.float32) * projected[u]
                part_ref[owner, f, iteration] = total

    def sweep(number, carry):
        receive(number)
        for some_neighbours in (neighbours[:2], neighbours[2:]):
            for k in some_neighbours:
                for h in range(halo):
                    fresh = jnp.concatenate(updated(want_ref[k, 0, h]), axis=0)
                    send_buf[lax.rem(number + 1, 2), k, h] = fresh.astype(jnp.bfloat16)
            for k in some_neighbours:
                halo_copy(number + 1, k).start()
        update_own()
        round_own()

        @pl.when(number == INNER - 1)
        def _():
            design(0)

        return carry

    lax.fori_loop(1, last, sweep, 0)
    receive(last)
    update_own()
    design(1)

    def sub_copy(d, f):
        other = lax.rem(s + d, n_sub)
        return pltpu.make_async_remote_copy(
            src_ref=part_ref.at[other, f], dst_ref=sub_buf.at[d - 1, f],
            send_sem=sub_send.at[d - 1, f], recv_sem=sub_recv.at[d - 1, f],
            device_id=(a, other), device_id_type=MESH)

    def dom_copy(k, f):
        return pltpu.make_async_remote_copy(
            src_ref=acc_ref.at[k, f], dst_ref=dom_buf.at[k, f],
            send_sem=dom_send.at[k, f], recv_sem=dom_recv.at[k, f],
            device_id=(partners[(k + f) % dom_steps], s), device_id_type=MESH)

    for f in range(fb_dev):
        for d in range(1, n_sub):
            sub_copy(d, f).start()
    for f in range(fb_dev):
        total = part_ref[s, f]
        for d in range(1, n_sub):
            sub_copy(d, f).wait()
            total = total + sub_buf[d - 1, f]
        acc_ref[0, f] = total
        dom_copy(0, f).start()
    for i in range(tiles):
        for v in range(NVAR):
            adj_out[i, pl.ds(v, NOBJ, stride=NVAR), :] = adj_ref[i, v]
    for k in range(dom_steps):
        for f in range(fb_dev):
            dom_copy(k, f).wait()
            total = acc_ref[k, f] + dom_buf[k, f]
            if k < dom_steps - 1:
                acc_ref[k + 1, f] = total
                dom_copy(k + 1, f).start()
            else:
                total = total * scaling
                for iteration in range(OUTER):
                    for x in range(NDIR):
                        grad_out[iteration, f, pl.ds(x, NOBJ, stride=NDIR), :] = (
                            total[iteration, x * NOBJ:(x + 1) * NOBJ])


def per_device(
    n_dom,
    n_sub,
    block_total,
    jac_blocks,
    block_cols,
    precond,
    right_side,
    halo_rows,
    surface_tile,
    surface_block,
    surface_count,
    surface_residual_derivative,
    lattice_bernstein_weights,
):
    tiles, blocks, cells, _ = jac_blocks.shape
    slots, controls, _ = lattice_bernstein_weights.shape
    neighbours, halo = halo_rows.shape
    fb_dev = block_total // n_sub
    rows = NOBJ * NVAR
    scaling = math.sqrt(fb_dev / (slots * n_dom))
    dom_steps = n_dom.bit_length() - 1
    grad_rows = NOBJ * NDIR
    f32, bf16, i32 = jnp.float32, jnp.bfloat16, jnp.int32
    dma = pltpu.SemaphoreType.DMA
    operands = (
        jac_blocks.reshape(tiles, blocks * cells, cells),
        precond,
        right_side,
        jnp.swapaxes(surface_residual_derivative, 0, 1),
        lattice_bernstein_weights,
        block_cols.T,
        halo_rows.T,
        surface_tile,
        surface_block,
        surface_count,
    )
    vmem = pl.BlockSpec(memory_space=pltpu.VMEM)
    return pl.pallas_call(
        functools.partial(kernel, n_dom, n_sub, scaling),
        out_shape=(
            jax.ShapeDtypeStruct((tiles, rows, cells), f32),
            jax.ShapeDtypeStruct((OUTER, fb_dev, grad_rows, controls), f32),
        ),
        in_specs=[pl.BlockSpec(memory_space=pltpu.HBM)] * len(operands),
        out_specs=(vmem, vmem),
        scratch_shapes=[pltpu.VMEM(x.shape, x.dtype) for x in operands[:5]]
        + [pltpu.SMEM(x.shape, x.dtype) for x in operands[5:]]
        + [
            pltpu.VMEM((tiles, NVAR * NVAR, NOBJ, cells), f32),
            pltpu.VMEM((tiles, NVAR, NOBJ, cells), f32),
            pltpu.VMEM((tiles, NVAR, NOBJ, cells), f32),
            pltpu.VMEM((tiles + neighbours * halo, rows, cells), bf16),
            pltpu.VMEM((2, neighbours, halo, rows, cells), bf16),
            pltpu.VMEM((2, neighbours, halo, rows, cells), bf16),
            pltpu.VMEM((neighbours, 8, 128), i32),
            pltpu.VMEM((neighbours, 8, 128), i32),
            pltpu.SMEM((neighbours, 8, 128), i32),
            pltpu.VMEM((n_sub, fb_dev, OUTER, grad_rows, controls), f32),
            pltpu.VMEM((n_sub - 1, fb_dev, OUTER, grad_rows, controls), f32),
            pltpu.VMEM((dom_steps, fb_dev, OUTER, grad_rows, controls), f32),
            pltpu.VMEM((dom_steps, fb_dev, OUTER, grad_rows, controls), f32),
            dma((len(operands),)),
            dma((neighbours,)),
            dma((neighbours,)),
            dma,
            dma((2, neighbours)),
            dma((2, neighbours)),
            dma((n_sub - 1, fb_dev)),
            dma((n_sub - 1, fb_dev)),
            dma((dom_steps, fb_dev)),
            dma((dom_steps, fb_dev)),
        ],
        compiler_params=pltpu.CompilerParams(
            collective_id=0, has_side_effects=True, vmem_limit_bytes=60 * 1024 * 1024),
    )(*operands)


FB_DEV = 4


def solution(mesh):
    n_dom, n_sub = mesh.shape["dom"], mesh.shape["sub"]
    both = ("dom", "sub")
    in_specs = (
        P(both, None, None, None),
        P(both, None),
        P(both, None, None),
        P(both, None, None),
        P(both, None),
        P(both),
        P(both),
        P(both),
        P(both, None, None),
        P(both, None, None),
    )
    out_specs = (P(both, None, None), P(None, "sub", None, None))
    return jax.shard_map(
        functools.partial(per_device, n_dom, n_sub, FB_DEV * n_sub),
        mesh=mesh, in_specs=in_specs, out_specs=out_specs, check_vma=False,
    )
```

```python
import functools
import math

import jax
import jax.numpy as jnp
from jax import lax
from jax.experimental import pallas as pl
from jax.experimental.pallas import tpu as pltpu
from jax.sharding import PartitionSpec as P

NOBJ = 8
NVAR = 6
NDIR = 3
OUTER = 2
INNER = 5

OFFSETS = (1, -1, 2, -2)
RELAXATION = 0.7
MESH = pl.DeviceIdType.MESH


def mixed(pre_ref, tile, residual):
    out = []
    for v in range(NVAR):
        total = RELAXATION * residual[v]
        for w in range(NVAR):
            total = total + pre_ref[tile, v * NVAR + w] * residual[w]
        out.append(total)
    return out


def kernel(
    n_dom, n_sub, scaling,
    jac_hbm, pre_hbm, rhs_hbm, srd_hbm, weights_hbm,
    cols_hbm, halo_hbm, surf_tile_hbm, surf_block_hbm, count_hbm,
    adj_out, grad_out,
    jac_ref, pre_in, rhs_in, srd_ref, weights_ref,
    cols_ref, halo_ref, surf_tile_ref, surf_block_ref, count_ref,
    pre_ref, rhs_ref, adj_ref, ext_ref, send_buf, recv_buf,
    want_out, want_in, want_ref,
    part_ref, sub_buf, acc_ref, dom_buf,
    load_sem, want_send, want_recv, want_local, halo_send, halo_recv,
    sub_send, sub_recv, dom_send, dom_recv,
):
    blocks, tiles = cols_ref.shape
    cells = adj_ref.shape[-1]
    halo = recv_buf.shape[2]
    slots = weights_ref.shape[0]
    fb_dev = grad_out.shape[1]
    rows = NOBJ * NVAR
    last = OUTER * INNER - 1
    neighbours = range(len(OFFSETS))
    a = lax.axis_index("dom")
    s = lax.axis_index("sub")

    def shifted(offset):
        return lax.rem(a + offset + n_dom, n_dom)

    pairs = {
        "halo": (halo_hbm, halo_ref), "rhs": (rhs_hbm, rhs_in), "pre": (pre_hbm, pre_in),
        "cols": (cols_hbm, cols_ref), "jac": (jac_hbm, jac_ref),
        "srd": (srd_hbm, srd_ref), "weights": (weights_hbm, weights_ref),
        "tile": (surf_tile_hbm, surf_tile_ref), "block": (surf_block_hbm, surf_block_ref),
        "count": (count_hbm, count_ref),
    }
    loads = {}
    for number, (name, (src, dst)) in enumerate(pairs.items()):
        loads[name] = pltpu.make_async_copy(src, dst, load_sem.at[number])

    dom_steps = n_dom.bit_length() - 1
    partners = [a + 2 ** k * (1 - 2 * lax.rem(a // 2 ** k, 2)) for k in range(dom_steps)]
    greet = [(shifted(offset), s) for offset in OFFSETS]
    greet += [(partners[k], s) for k in range(2, dom_steps)]
    greet += [(a, lax.rem(s + d, n_sub)) for d in range(1, n_sub)]
    barrier = pltpu.get_barrier_semaphore()
    for device in greet:
        pl.semaphore_signal(barrier, inc=1, device_id=device, device_id_type=MESH)
    for load in loads.values():
        load.start()

    loads["halo"].wait()
    lane = lax.broadcasted_iota(jnp.int32, want_out.shape[1:], 1)
    for k in neighbours:
        demand = jnp.zeros(want_out.shape[1:], jnp.int32)
        for h in range(halo):
            demand = jnp.where(lane == h, halo_ref[h, k], demand)
        want_out[k] = demand
    pl.semaphore_wait(barrier, len(greet))

    def want_copy(k):
        return pltpu.make_async_remote_copy(
            src_ref=want_out.at[k], dst_ref=want_in.at[k],
            send_sem=want_send.at[k], recv_sem=want_recv.at[k],
            device_id=(shifted(-OFFSETS[k]), s), device_id_type=MESH)

    for k in neighbours:
        want_copy(k).start()

    loads["rhs"].wait()
    loads["pre"].wait()

    def first(i, carry):
        for row in range(NVAR * NVAR):
            spread = jnp.broadcast_to(pre_in[i, pl.ds(row, 1), :], (NOBJ, cells))
            pre_ref[i, row] = spread
        residual = []
        for v in range(NVAR):
            value = rhs_in[i, pl.ds(v, NOBJ, stride=NVAR), :]
            rhs_ref[i, v] = value
            residual.append(value)
        for v, change in enumerate(mixed(pre_ref, i, residual)):
            adj_ref[i, v] = change
        return carry

    lax.fori_loop(0, tiles, first, 0)

    def halo_copy(number, k):
        parity = lax.rem(number, 2)
        return pltpu.make_async_remote_copy(
            src_ref=send_buf.at[parity, k], dst_ref=recv_buf.at[parity, k],
            send_sem=halo_send.at[parity, k], recv_sem=halo_recv.at[parity, k],
            device_id=(shifted(OFFSETS[k]), s), device_id_type=MESH)

    def round_own():
        for i in range(tiles):
            ext_ref[i] = adj_ref[i].reshape(rows, cells).astype(jnp.bfloat16)

    for k in neighbours:
        want_copy(k).wait()
    to_smem = pltpu.make_async_copy(want_in, want_ref, want_local)
    to_smem.start()
    to_smem.wait()
    for k in neighbours:
        for h in range(halo):
            tile = adj_ref[want_ref[k, 0, h]]
            send_buf[1, k, h] = tile.reshape(rows, cells).astype(jnp.bfloat16)
        halo_copy(1, k).start()
    round_own()
    for name in ("cols", "jac", "srd", "weights", "tile", "block", "count"):
        loads[name].wait()

    def updated(i):
        picked = jnp.concatenate([ext_ref[cols_ref[b, i]] for b in range(blocks)], axis=1)
        product = jnp.dot(picked, jac_ref[i], preferred_element_type=jnp.float32)
        current = [adj_ref[i, v] for v in range(NVAR)]
        residual = [
            rhs_ref[i, v] - (current[v] + product[v * NOBJ:(v + 1) * NOBJ]) for v in range(NVAR)
        ]
        return [c + change for c, change in zip(current, mixed(pre_ref, i, residual))]

    def update_own():
        for i in range(tiles):
            for v, value in enumerate(updated(i)):
                adj_ref[i, v] = value

    def receive(number):
        parity = lax.rem(number, 2)
        for k in neighbours:
            halo_copy(number, k).wait()
        for k in neighbours:
            for h in range(halo):
                ext_ref[tiles + k * halo + h] = recv_buf[parity, k, h]

    def design(iteration):
        projected = []
        for u in range(slots):
            alive = jnp.where(u < count_ref[0], 1.0, 0.0).astype(jnp.float32)
            selected = adj_ref[surf_tile_ref[u]]
            parts = []
            for k in range(NDIR):
                total = selected[0] * srd_ref[k, pl.ds(u, 1), :]
                for v in range(1, NVAR):
                    total = total + selected[v] * srd_ref[v * NDIR + k, pl.ds(u, 1), :]
                parts.append(total * alive)
            rounded = jnp.concatenate(parts, axis=0).astype(jnp.bfloat16)
            projected.append(lax.dot_general(
                rounded, weights_ref[u], (((1,), (1,)), ((), ())),
                preferred_element_type=jnp.float32))
        for owner in range(n_sub):
            for f in range(fb_dev):
                total = jnp.zeros_like(projected[0])
                for u in range(slots):
                    chosen = jnp.where(surf_block_ref[u] == owner * fb_dev + f, 1.0, 0.0)
                    total = total + chosen.astype(jnp.float32) * projected[u]
                part_ref[iteration, owner, f] = total

    def sub_copy(iteration, d, f):
        other = lax.rem(s + d, n_sub)
        return pltpu.make_async_remote_copy(
            src_ref=part_ref.at[iteration, other, f], dst_ref=sub_buf.at[iteration, d - 1, f],
            send_sem=sub_send.at[iteration, d - 1, f], recv_sem=sub_recv.at[iteration, d - 1, f],
            device_id=(a, other), device_id_type=MESH)

    def dom_copy(iteration, k, f):
        return pltpu.make_async_remote_copy(
            src_ref=acc_ref.at[iteration, k, f], dst_ref=dom_buf.at[iteration, k, f],
            send_sem=dom_send.at[iteration, k, f], recv_sem=dom_recv.at[iteration, k, f],
            device_id=(partners[(k + f) % dom_steps], s), device_id_type=MESH)

    def send_partials(iteration):
        for f in range(fb_dev):
            for d in range(1, n_sub):
                sub_copy(iteration, d, f).start()

    def finish_stage(iteration, stage):
        for f in range(fb_dev):
            if stage == 0:
                total = part_ref[iteration, s, f]
                for d in range(1, n_sub):
                    sub_copy(iteration, d, f).wait()
                    total = total + sub_buf[iteration, d - 1, f]
            else:
                dom_copy(iteration, stage - 1, f).wait()
                total = acc_ref[iteration, stage - 1, f] + dom_buf[iteration, stage - 1, f]
            if stage < dom_steps:
                acc_ref[iteration, stage, f] = total
                dom_copy(iteration, stage, f).start()
            else:
                total = total * scaling
                for x in range(NDIR):
                    grad_out[iteration, f, pl.ds(x, NOBJ, stride=NDIR), :] = (
                        total[x * NOBJ:(x + 1) * NOBJ])

    beside = min(dom_steps + 1, last - INNER)

    def sweep(number, carry):
        receive(number)
        for stage in range(beside):
            @pl.when(number == INNER + stage)
            def _():
                finish_stage(0, stage)

        for some_neighbours in (neighbours[:2], neighbours[2:]):
            for k in some_neighbours:
                for h in range(halo):
                    fresh = jnp.concatenate(updated(want_ref[k, 0, h]), axis=0)
                    send_buf[lax.rem(number + 1, 2), k, h] = fresh.astype(jnp.bfloat16)
            for k in some_neighbours:
                halo_copy(number + 1, k).start()
        update_own()
        round_own()

        @pl.when(number == INNER - 1)
        def _():
            design(0)
            send_partials(0)

        return carry

    lax.fori_loop(1, last, sweep, 0)
    receive(last)
    update_own()
    design(1)
    send_partials(1)
    for i in range(tiles):
        for v in range(NVAR):
            adj_out[i, pl.ds(v, NOBJ, stride=NVAR), :] = adj_ref[i, v]
    for stage in range(beside, dom_steps + 1):
        finish_stage(0, stage)
    for stage in range(dom_steps + 1):
        finish_stage(1, stage)


def per_device(
    n_dom,
    n_sub,
    block_total,
    jac_blocks,
    block_cols,
    precond,
    right_side,
    halo_rows,
    surface_tile,
    surface_block,
    surface_count,
    surface_residual_derivative,
    lattice_bernstein_weights,
):
    tiles, blocks, cells, _ = jac_blocks.shape
    slots, controls, _ = lattice_bernstein_weights.shape
    neighbours, halo = halo_rows.shape
    fb_dev = block_total // n_sub
    rows = NOBJ * NVAR
    scaling = math.sqrt(fb_dev / (slots * n_dom))
    dom_steps = n_dom.bit_length() - 1
    grad_rows = NOBJ * NDIR
    f32, bf16, i32 = jnp.float32, jnp.bfloat16, jnp.int32
    dma = pltpu.SemaphoreType.DMA
    operands = (
        jac_blocks.reshape(tiles, blocks * cells, cells),
        precond,
        right_side,
        jnp.swapaxes(surface_residual_derivative, 0, 1),
        lattice_bernstein_weights,
        block_cols.T,
        halo_rows.T,
        surface_tile,
        surface_block,
        surface_count,
    )
    vmem = pl.BlockSpec(memory_space=pltpu.VMEM)
    return pl.pallas_call(
        functools.partial(kernel, n_dom, n_sub, scaling),
        out_shape=(
            jax.ShapeDtypeStruct((tiles, rows, cells), f32),
            jax.ShapeDtypeStruct((OUTER, fb_dev, grad_rows, controls), f32),
        ),
        in_specs=[pl.BlockSpec(memory_space=pltpu.HBM)] * len(operands),
        out_specs=(vmem, vmem),
        scratch_shapes=[pltpu.VMEM(x.shape, x.dtype) for x in operands[:5]]
        + [pltpu.SMEM(x.shape, x.dtype) for x in operands[5:]]
        + [
            pltpu.VMEM((tiles, NVAR * NVAR, NOBJ, cells), f32),
            pltpu.VMEM((tiles, NVAR, NOBJ, cells), f32),
            pltpu.VMEM((tiles, NVAR, NOBJ, cells), f32),
            pltpu.VMEM((tiles + neighbours * halo, rows, cells), bf16),
            pltpu.VMEM((2, neighbours, halo, rows, cells), bf16),
            pltpu.VMEM((2, neighbours, halo, rows, cells), bf16),
            pltpu.VMEM((neighbours, 8, 128), i32),
            pltpu.VMEM((neighbours, 8, 128), i32),
            pltpu.SMEM((neighbours, 8, 128), i32),
            pltpu.VMEM((OUTER, n_sub, fb_dev, grad_rows, controls), f32),
            pltpu.VMEM((OUTER, n_sub - 1, fb_dev, grad_rows, controls), f32),
            pltpu.VMEM((OUTER, dom_steps, fb_dev, grad_rows, controls), f32),
            pltpu.VMEM((OUTER, dom_steps, fb_dev, grad_rows, controls), f32),
            dma((len(operands),)),
            dma((neighbours,)),
            dma((neighbours,)),
            dma,
            dma((2, neighbours)),
            dma((2, neighbours)),
            dma((OUTER, n_sub - 1, fb_dev)),
            dma((OUTER, n_sub - 1, fb_dev)),
            dma((OUTER, dom_steps, fb_dev)),
            dma((OUTER, dom_steps, fb_dev)),
        ],
        compiler_params=pltpu.CompilerParams(
            collective_id=0, has_side_effects=True, vmem_limit_bytes=60 * 1024 * 1024),
    )(*operands)


FB_DEV = 4


def solution(mesh):
    n_dom, n_sub = mesh.shape["dom"], mesh.shape["sub"]
    both = ("dom", "sub")
    in_specs = (
        P(both, None, None, None),
        P(both, None),
        P(both, None, None),
        P(both, None, None),
        P(both, None),
        P(both),
        P(both),
        P(both),
        P(both, None, None),
        P(both, None, None),
    )
    out_specs = (P(both, None, None), P(None, "sub", None, None))
    return jax.shard_map(
        functools.partial(per_device, n_dom, n_sub, FB_DEV * n_sub),
        mesh=mesh, in_specs=in_specs, out_specs=out_specs, check_vma=False,
    )
```
